512 devices in a mesh: hist: 128 (over z, y, core), col: 4 (over x).
Axes of the slice: x: 4, y: 8, z: 8, core: 2. Of those that a mesh axis runs over, the one named last changes fastest.
Arguments:
- sigma_ret: bfloat16 [4, 512, 64, 128], P(None, 'hist', 'col'), may hold values from -6 to 6
- sigma_less: bfloat16 [4, 512, 64, 128], P(None, 'hist', 'col'), may hold values from -6 to 6
- green_less: bfloat16 [512, 96, 64, 128], P('hist', 'col'), may hold values from -0.0234375 to 0.0234375
- green_adv: bfloat16 [512, 96, 64, 128], P('hist', 'col'), may hold values from -0.0234375 to 0.0234375
- time_now: int32 [4], replicated, may hold values from 256 to 511, as said below
- col_start: int32 [96], P('col'), may hold values from 0 to 255
Outputs:
- collision: bfloat16 [4, 96, 64, 128], P(None, 'col')
The draws below stay inside these ranges and needn't reach their ends.
Inputs may be any that keep to these rules, and one draw needn't show every extreme that they name: Some time row has time_now = 511.
All inputs are finite; a program needn't handle non-finite values.
Results may differ from the reference program's by a relative error of at most 0.001.
Values may be sent and summed in bfloat16 or wider, within the bound.
A program may use at most 64 MiB of HBM per device.

```python
import jax
import jax.numpy as jnp
from jax import lax

NORB = 64
NT = 4
TB = 512
TC = 96


def draw_time_now(key, part):
    key = jax.random.fold_in(key, 7)
    key_vals = jax.random.fold_in(key, 1)
    key_pick = jax.random.fold_in(key, 2)
    values = jax.random.randint(key_vals, (NT,), TB // 2, TB, dtype=jnp.int32)
    picked = jax.random.randint(key_pick, (), 0, NT, dtype=jnp.int32)
    rows = jnp.arange(NT, dtype=jnp.int32)
    return jnp.where(rows == picked, jnp.int32(TB - 1), values).astype(jnp.int32)


def touch_ends(drawn, stream_key, low, high):
    longest = drawn.shape.index(max(drawn.shape))
    spots = []
    for shift in (0, 1):
        where = [jax.random.randint(jax.random.fold_in(stream_key, axis), (), 0, length) for axis, length in enumerate(drawn.shape)]
        where[longest] = (where[longest] + shift) % drawn.shape[longest]
        spots.append(tuple(where))
    return drawn.at[spots[0]].set(low).at[spots[1]].set(high)


def level_of(rng, shape, cuts, least, largest):
    gain, own = 1.0, jax.random.fold_in(rng, 6)
    for axis_at, blocks in cuts:
        steps = jnp.exp(jax.random.uniform(jax.random.fold_in(own, axis_at), (blocks,), jnp.float32, least / len(cuts), largest / len(cuts)))
        gain = gain * jnp.repeat(steps, shape[axis_at] // blocks).reshape([-1 if axis == axis_at else 1 for axis in range(len(shape))])
    return gain


def centred(rng, extent, spread, most, pieces=(), kind=jnp.bfloat16):
    result = jax.random.normal(rng, extent, jnp.float32) * spread
    if len(pieces) > 0:
        result = level_of(rng, extent, pieces, -0.22, 0.18) * result
    return jnp.clip(result, min=-most, max=most).astype(kind)


def setup_inputs(seed: int = 0) -> dict:
    arg_keys = jax.random.split(jax.random.key(seed), 7)
    return {
        "sigma_ret": centred(arg_keys[0], (NT, TB, NORB, 2 * NORB), 1.0, 6.0, ((1, 128), (2, 4))),
        "sigma_less": centred(arg_keys[1], (NT, TB, NORB, 2 * NORB), 1.0, 6.0, ((1, 128), (2, 4))),
        "green_less": centred(arg_keys[2], (TB, TC, NORB, 2 * NORB), (2 * TB * NORB) ** -0.5, 0.0234375, ((0, 128), (1, 4))),
        "green_adv": centred(arg_keys[3], (TB, TC, NORB, 2 * NORB), (2 * TB * NORB) ** -0.5, 0.0234375, ((0, 128), (1, 4))),
        "time_now": draw_time_now(jax.random.fold_in(arg_keys[6], 71), 0),
        "col_start": touch_ends(jax.random.randint(arg_keys[5], (TC,), 0, TB // 2), jax.random.fold_in(arg_keys[5], 1), 0, (TB // 2) - 1).astype(jnp.int32),
    }


def widen(green):
    real_part = green[..., :NORB]
    imag_part = green[..., NORB:]
    lower = jnp.concatenate([-imag_part, real_part], axis=-1)
    return jnp.concatenate([green, lower], axis=-2)


def reference(sigma_ret, sigma_less, green_less, green_adv, time_now, col_start):
    tbar = jnp.arange(TB, dtype=jnp.int32)
    before = (tbar[None, :] <= time_now[:, None])[:, :, None, None]
    left_r = jnp.where(before, sigma_ret.astype(jnp.float32), 0.0)
    left_l = jnp.where(before, sigma_less.astype(jnp.float32), 0.0)

    def one_column(column):
        g_less, g_adv, start = column
        after = (tbar >= start)[:, None, None]
        b_less = jnp.where(after, widen(g_less.astype(jnp.float32)), 0.0)
        b_adv = jnp.where(after, widen(g_adv.astype(jnp.float32)), 0.0)
        first = jnp.einsum("tbik,bkn->tin", left_r, b_less, precision=lax.Precision.HIGHEST)
        second = jnp.einsum("tbik,bkn->tin", left_l, b_adv, precision=lax.Precision.HIGHEST)
        return first + second

    cols = lax.map(one_column, (jnp.swapaxes(green_less, 0, 1), jnp.swapaxes(green_adv, 0, 1), col_start))
    return jnp.swapaxes(cols, 0, 1).astype(jnp.bfloat16)
```

```python
import functools

import jax
import jax.numpy as jnp
from jax import lax
from jax.experimental import pallas as pl
from jax.experimental.pallas import tpu as pltpu
from jax.sharding import PartitionSpec as P

MESH = pl.DeviceIdType.MESH
RING = 8
COLS = 12
STEP = (0, 1, 3, 2)


def kernel(time_ref, start_ref, sr_ref, sl_ref, gl_ref, ga_ref, out_ref,
           raw, left, green, c_send, c_recv, part, coded, scale, rx_p, rx_q, sc_p, sc_q, sum_p, sum_q, own_p, own_q,
           in_sem, x_s, x_r, c_s, c_r, r1_s, r1_r, k_s, k_r, r2p_s, r2q_s, r2p_r, r2q_r,
           a1p_s, a1q_s, a1p_r, a1q_r, a2_s, a2_r, f_s, f_r):
    hist, x = lax.axis_index("hist"), lax.axis_index("col")
    core = hist % 2
    z, y = hist // 16, (hist // 2) % 8
    a = y * (1 - core) + z * core
    b = z * (1 - core) + y * core
    step_a, step_b = 2 + 14 * core, 16 - 14 * core
    base = COLS * core
    other = COLS * (1 - core)

    def at_a(pos):
        return (pos * step_a + b * step_b + core, x)

    def at_b(pos):
        return (a * step_a + pos * step_b + core, x)

    def at_x(pos):
        return (hist, pos)

    sibling = (hist + 1 - 2 * core, x)

    def remote(src, dst, send, recv, device):
        return pltpu.make_async_remote_copy(
            src_ref=src, dst_ref=dst, send_sem=send, recv_sem=recv, device_id=device, device_id_type=MESH
        )

    loads = [pltpu.make_async_copy(sr_ref, raw.at[0], in_sem.at[0]), pltpu.make_async_copy(sl_ref, raw.at[1], in_sem.at[1])]
    for half, first in ((0, other), (1, base)):
        for term, ref in ((0, gl_ref), (1, ga_ref)):
            columns = pl.ds(first, COLS)
            loads.append(pltpu.make_async_copy(ref.at[:, columns], green.at[term, :, columns], in_sem.at[2 + 2 * half + term]))
    for load in loads:
        load.start()

    barrier = pltpu.get_barrier_semaphore()

    def hail(device):
        pl.semaphore_signal(barrier, inc=1, device_id=device, device_id_type=MESH)

    hail(sibling)
    for j in (1, 2, 3):
        hail(at_x((x + j) % 4))

    def hail_rings(d, carry):
        hail(at_a((a + d) % RING))
        hail(at_b((b + d) % RING))
        return carry

    lax.fori_loop(1, RING, hail_rings, 0)

    loads[0].wait()
    loads[1].wait()
    low = lax.broadcasted_iota(jnp.int32, (16, 128), 1) < 64
    for term in range(2):
        for t in range(4):
            now = time_ref[t]
            for pair in range(2):
                v = []
                for k in range(2):
                    tb = 2 * pair + k
                    value = raw[term, t, tb].astype(jnp.float32)
                    v.append(jnp.where(hist * 4 + tb <= now, value, jnp.zeros_like(value)))
                depth = slice(128 * pair, 128 * pair + 128)
                re = jnp.where(low, v[0], pltpu.roll(v[1], 64, 1))
                im = jnp.where(low, pltpu.roll(v[0], 64, 1), v[1])
                left[term, 0, 16 * t : 16 * t + 16, depth] = re.astype(jnp.bfloat16)
                left[term, 0, 64 + 16 * t : 80 + 16 * t, depth] = im.astype(jnp.bfloat16)

    sign = jnp.where(lax.broadcasted_iota(jnp.int32, (64, 128), 1) < 64, -1.0, 1.0).astype(jnp.float32)

    def products(first_stage, n, first_col, target, masked):
        def two(j, carry):
            rights = []
            for term in range(2):
                columns = []
                for k in range(2):
                    c = first_col + 2 * j + k
                    rows = []
                    for tb in range(4):
                        g = green[term, tb, c]
                        if not masked:
                            g = jnp.where(hist * 4 + tb >= start_ref[c], g, jnp.zeros_like(g))
                            green[term, tb, c] = g
                        rows.append(g)
                    columns.append(jnp.concatenate(rows, axis=0))
                rights.append(jnp.concatenate(columns, axis=1))
            acc = None
            for term in range(2):
                lhs = left[term, first_stage : first_stage + n].reshape(n * 128, 256)
                d = jnp.dot(lhs, rights[term], preferred_element_type=jnp.float32)
                acc = d if acc is None else acc + d
            for i in range(n):
                for k in range(2):
                    one = acc[128 * i : 128 * i + 64, 128 * k : 128 * k + 128]
                    two_ = acc[128 * i + 64 : 128 * i + 128, 128 * k : 128 * k + 128]
                    value = one + pltpu.roll(two_, 64, 1) * sign
                    target[first_stage + i, 2 * j + k] = value.reshape(4, 16, 128)
            return carry

        lax.fori_loop(0, COLS // 2, two, 0)

    def pair_copy(s, n):
        at = pl.ds(s, n)
        return remote(c_send.at[at], c_recv.at[at], c_s.at[s], c_r.at[s], sibling)

    def encode(s):
        def add(c, most):
            v = part[s, c] + c_recv[s, c]
            part[s, c] = v
            return jnp.maximum(most, jnp.max(jnp.abs(v).reshape(8, 8, 128), axis=0))

        most = lax.fori_loop(0, COLS, add, jnp.zeros((8, 128), jnp.float32))
        most = jnp.maximum(jnp.max(most, axis=0, keepdims=True), 1e-33)
        scale[s] = most * (1.0 / 32767.0)
        factor = (32767.0 / most).reshape(1, 1, 128)

        def code(c, carry):
            coded[s, c] = jnp.round(part[s, c] * factor).astype(jnp.int32).astype(jnp.int16)
            return carry

        lax.fori_loop(0, COLS, code, 0)

    def ring_one(s):
        def send(d, carry):
            i = (a + d) % RING
            remote(coded.at[s, i], rx_p.at[s, d - 1], r1_s.at[s, 0], r1_r.at[s, 0], at_a(i)).start()
            remote(scale.at[s], sc_p.at[s, d - 1], k_s.at[s, 0], k_r.at[s, 0], at_a(i)).start()
            i = (b + d) % RING
            remote(coded.at[s, 8 + i // 2, pl.ds(2 * (i % 2), 2)], rx_q.at[s, d - 1], r1_s.at[s, 1], r1_r.at[s, 1], at_b(i)).start()
            remote(scale.at[s], sc_q.at[s, d - 1], k_s.at[s, 1], k_r.at[s, 1], at_b(i)).start()
            return carry

        lax.fori_loop(1, RING, send, 0)

    def ring_one_all(s):
        return [
            remote(rx_p.at[s], rx_p.at[s], r1_s.at[s, 0], r1_r.at[s, 0], sibling),
            remote(sc_p.at[s], sc_p.at[s], k_s.at[s, 0], k_r.at[s, 0], sibling),
            remote(rx_q.at[s], rx_q.at[s], r1_s.at[s, 1], r1_r.at[s, 1], sibling),
            remote(sc_q.at[s], sc_q.at[s], k_s.at[s, 1], k_r.at[s, 1], sibling),
        ]

    def p_copy(s, k):
        o = 4 * (s % 2) + k
        return o, remote(sum_p.at[s, k], own_p.at[s // 2, (b - o + RING) % RING - 1], r2p_s.at[s, k], r2p_r.at[s // 2], at_b(o))

    def q_copy(s, k):
        o = 2 * s + k
        return o, remote(sum_q.at[s, k], own_q.at[(a - o + RING) % RING - 1], r2q_s.at[s, k], r2q_r.at[0], at_a(o))

    def ring_two(s):
        for copy in ring_one_all(s):
            copy.wait_recv()
        total = part[s, a]
        for d in range(RING - 1):
            total = total + rx_p[s, d].astype(jnp.int32).astype(jnp.float32) * sc_p[s, d].reshape(1, 1, 128)
        sum_p[s] = total
        total = part[s, 8 + b // 2, pl.ds(2 * (b % 2), 2)]
        for d in range(RING - 1):
            total = total + rx_q[s, d].astype(jnp.int32).astype(jnp.float32) * sc_q[s, d].reshape(1, 1, 128)
        sum_q[s] = total
        for k in range(4):
            o, copy = p_copy(s, k)
            pl.when(o != b)(copy.start)
        for k in range(2):
            o, copy = q_copy(s, k)
            pl.when(o != a)(copy.start)

    def rows_of(s):
        return (x + STEP[s]) % 4

    def p_tile(s, k):
        return out_ref.at[k, base + a, rows_of(s)]

    def q_tile(s, k):
        return out_ref.at[2 * (b % 2) + k, base + 8 + b // 2, rows_of(s)]

    def own(s):
        @pl.when(b // 4 == s % 2)
        def _():
            u = s // 2
            remote(own_p.at[u], own_p.at[u], r2p_s.at[s, 0], r2p_r.at[u], sibling).wait_recv()
            total = sum_p[s, b % 4]
            for d in range(RING - 1):
                total = total + own_p[u, d]
            tile = p_tile(s, b % 4)
            tile[...] = total.astype(jnp.bfloat16)

            def send(d, carry):
                remote(tile, tile, a1p_s.at[u], a1p_r.at[s, b % 4], at_b((b + d) % RING)).start()
                return carry

            lax.fori_loop(1, RING, send, 0)

        @pl.when(a // 2 == s)
        def _():
            remote(own_q, own_q, r2q_s.at[s, 0], r2q_r.at[0], sibling).wait_recv()
            total = sum_q[s, a % 2]
            for d in range(RING - 1):
                total = total + own_q[d]
            tile = q_tile(s, a % 2)
            tile[...] = total.astype(jnp.bfloat16)

            def send(d, carry):
                remote(tile, tile, a1q_s.at[0], a1q_r.at[s, a % 2], at_a((a + d) % RING)).start()
                return carry

            lax.fori_loop(1, RING, send, 0)

    def spread(s):
        for k in range(4):
            tile = p_tile(s, k)
            copy = remote(tile, tile, a1p_s.at[0], a1p_r.at[s, k], sibling)
            pl.when(4 * (s % 2) + k != b)(copy.wait_recv)
        mine = out_ref.at[:, base + a, rows_of(s)]

        def send_p(d, carry):
            remote(mine, mine, a2_s.at[s, 0], a2_r.at[s, 0], at_a((a + d) % RING)).start()
            return carry

        lax.fori_loop(1, RING, send_p, 0)
        for k in range(2):
            tile = q_tile(s, k)
            copy = remote(tile, tile, a1q_s.at[0], a1q_r.at[s, k], sibling)
            pl.when(2 * s + k != a)(copy.wait_recv)
        my_q = out_ref.at[pl.ds(2 * (b % 2), 2), base + 8 + b // 2, rows_of(s)]

        def send_q(d, carry):
            remote(my_q, my_q, a2_s.at[s, 1], a2_r.at[s, 1], at_b((b + d) % RING)).start()
            return carry

        lax.fori_loop(1, RING, send_q, 0)

    def spread_all(s):
        p = out_ref.at[:, pl.ds(base, 7), rows_of(s)]
        q = out_ref.at[pl.ds(0, 2), pl.ds(base, 7), rows_of(s)]
        return [remote(p, p, a2_s.at[s, 0], a2_r.at[s, 0], sibling), remote(q, q, a2_s.at[s, 1], a2_r.at[s, 1], sibling)]

    def hand_over(s):
        mine = out_ref.at[:, pl.ds(base, COLS), rows_of(s)]
        return remote(mine, mine, f_s.at[s], f_r.at[s], sibling)

    def forward(s):
        for copy in spread_all(s):
            copy.wait_recv()
        hand_over(s).start()

    def quarter(stage):
        return remote(left.at[:, 0], left.at[:, stage], x_s.at[stage - 1], x_r.at[stage - 1], at_x((x + 4 - STEP[stage]) % 4))

    loads[2].wait()
    loads[3].wait()
    products(0, 1, other, c_send, False)
    pl.semaphore_wait(barrier, 18)
    for stage in (1, 2, 3):
        quarter(stage).start()
    pair_copy(0, 1).start()
    loads[4].wait()
    loads[5].wait()
    products(0, 1, base, part, False)
    pair_copy(0, 1).wait_recv()
    encode(0)
    ring_one(0)
    quarter(1).wait_recv()
    quarter(2).wait_recv()
    products(1, 2, other, c_send, True)
    pair_copy(1, 2).start()
    products(1, 2, base, part, True)
    pair_copy(1, 2).wait_recv()
    for s in (1, 2):
        encode(s)
        ring_one(s)
    ring_two(0)
    quarter(3).wait_recv()
    products(3, 1, other, c_send, True)
    pair_copy(3, 1).start()
    products(3, 1, base, part, True)
    pair_copy(3, 1).wait_recv()
    encode(3)
    ring_one(3)
    own(0)
    ring_two(1)
    ring_two(2)
    ring_two(3)
    spread(0)
    own(1)
    own(2)
    own(3)
    spread(1)
    forward(0)
    spread(2)
    spread(3)
    for s in (1, 2, 3):
        forward(s)
    for s in range(4):
        hand_over(s).wait_recv()

    for stage in (1, 2, 3):
        quarter(stage).wait_send()
    for s, n in ((0, 1), (1, 2), (3, 1)):
        pair_copy(s, n).wait_send()
    for s in range(4):
        for copy in ring_one_all(s):
            copy.wait_send()
        for k in range(4):
            o, copy = p_copy(s, k)
            pl.when(o != b)(copy.wait_send)
        for k in range(2):
            o, copy = q_copy(s, k)
            pl.when(o != a)(copy.wait_send)
        for copy in spread_all(s):
            copy.wait_send()
        hand_over(s).wait_send()
    seven = out_ref.at[0, pl.ds(0, 7), 0]
    for u in range(2):
        remote(seven, seven, a1p_s.at[u], a1p_r.at[0, 0], sibling).wait_send()
    remote(seven, seven, a1q_s.at[0], a1q_r.at[0, 0], sibling).wait_send()


def on_device(sigma_ret, sigma_less, green_less, green_adv, time_now, col_start):
    dma = pltpu.SemaphoreType.DMA
    f32, bf16, i16 = jnp.float32, jnp.bfloat16, jnp.int16
    out = pl.pallas_call(
        kernel,
        out_shape=jax.ShapeDtypeStruct((4, 24, 4, 16, 128), bf16),
        in_specs=[pl.BlockSpec(memory_space=pltpu.SMEM)] * 2 + [pl.BlockSpec(memory_space=pl.ANY)] * 4,
        out_specs=pl.BlockSpec(memory_space=pltpu.VMEM),
        scratch_shapes=[
            pltpu.VMEM((2, 4, 4, 16, 128), bf16),
            pltpu.VMEM((2, 4, 128, 256), bf16),
            pltpu.VMEM((2, 4, 24, 64, 128), bf16),
            pltpu.VMEM((4, COLS, 4, 16, 128), f32),
            pltpu.VMEM((4, COLS, 4, 16, 128), f32),
            pltpu.VMEM((4, COLS, 4, 16, 128), f32),
            pltpu.VMEM((4, COLS, 4, 16, 128), i16),
            pltpu.VMEM((4, 1, 128), f32),
            pltpu.VMEM((4, 7, 4, 16, 128), i16),
            pltpu.VMEM((4, 7, 2, 16, 128), i16),
            pltpu.VMEM((4, 7, 1, 128), f32),
            pltpu.VMEM((4, 7, 1, 128), f32),
            pltpu.VMEM((4, 4, 16, 128), f32),
            pltpu.VMEM((4, 2, 16, 128), f32),
            pltpu.VMEM((2, 7, 16, 128), f32),
            pltpu.VMEM((7, 16, 128), f32),
            dma((6,)),
            dma((3,)), dma((3,)),
            dma((4,)), dma((4,)),
            dma((4, 2)), dma((4, 2)),
            dma((4, 2)), dma((4, 2)),
            dma((4, 4)), dma((4, 2)), dma((2,)), dma((1,)),
            dma((2,)), dma((1,)), dma((4, 4)), dma((4, 2)),
            dma((4, 2)), dma((4, 2)),
            dma((4,)), dma((4,)),
        ],
        compiler_params=pltpu.CompilerParams(collective_id=0, has_side_effects=True, vmem_limit_bytes=40 * 1024 * 1024),
        cost_estimate=pl.CostEstimate(flops=1_610_612_736, bytes_accessed=5_000_000, transcendentals=0),
    )(time_now, col_start, sigma_ret, sigma_less, green_less, green_adv)
    return out.reshape(4, 24, 64, 128)


def solution(mesh):
    return jax.shard_map(
        on_device,
        mesh=mesh,
        in_specs=(
            P(None, "hist", "col", None),
            P(None, "hist", "col", None),
            P("hist", "col", None, None),
            P("hist", "col", None, None),
            P(),
            P("col"),
        ),
        out_specs=P(None, "col", None, None),
        check_vma=False,
    )
```

```python
import functools

import jax
import jax.numpy as jnp
from jax import lax
from jax.experimental import pallas as pl
from jax.experimental.pallas import tpu as pltpu
from jax.sharding import PartitionSpec as P

MESH = pl.DeviceIdType.MESH
RING = 8
COLS = 12
STEP = (0, 1, 3, 2)


def kernel(time_ref, start_ref, sr_ref, sl_ref, gl_ref, ga_ref, out_ref,
           times, starts, raw, left, green, out, c_send, c_recv, part, coded, scale, rx_p, rx_q, sc_p, sc_q, xp, xq, kp, kq,
           in_sem, x_s, x_r, c_s, c_r, r1_s, r1_r, k_s, k_r, r2_s, r2_r, k2_s, k2_r,
           a2_s, a2_r, f_s, f_r, l_s):
    hist, x = lax.axis_index("hist"), lax.axis_index("col")
    core = hist % 2
    z, y = hist // 16, (hist // 2) % 8
    a = y * (1 - core) + z * core
    b = z * (1 - core) + y * core
    step_a, step_b = 2 + 14 * core, 16 - 14 * core
    base = COLS * core
    other = COLS * (1 - core)

    def at_a(pos):
        return (pos * step_a + b * step_b + core, x)

    def at_b(pos):
        return (a * step_a + pos * step_b + core, x)

    def at_x(pos):
        return (hist, pos)

    sibling = (hist + 1 - 2 * core, x)

    def remote(src, dst, send, recv, device):
        return pltpu.make_async_remote_copy(
            src_ref=src, dst_ref=dst, send_sem=send, recv_sem=recv, device_id=device, device_id_type=MESH
        )

    small = [
        pltpu.make_async_copy(time_ref, times, in_sem.at[6]),
        pltpu.make_async_copy(start_ref, starts, in_sem.at[7]),
    ]
    loads = [pltpu.make_async_copy(sr_ref, raw.at[0], in_sem.at[0]), pltpu.make_async_copy(sl_ref, raw.at[1], in_sem.at[1])]
    for half, first in ((0, other), (1, base)):
        for term, ref in ((0, gl_ref), (1, ga_ref)):
            columns = pl.ds(first, COLS)
            loads.append(pltpu.make_async_copy(ref.at[:, columns], green.at[term, :, columns], in_sem.at[2 + 2 * half + term]))
    for load in loads[:2] + small + loads[2:]:
        load.start()

    barrier = pltpu.get_barrier_semaphore()

    def hail(device):
        pl.semaphore_signal(barrier, inc=1, device_id=device, device_id_type=MESH)

    hail(sibling)
    for j in (1, 2, 3):
        hail(at_x((x + j) % 4))

    def hail_rings(d, carry):
        hail(at_a((a + d) % RING))
        hail(at_b((b + d) % RING))
        return carry

    lax.fori_loop(1, RING, hail_rings, 0)

    for load in loads[:2] + small:
        load.wait()
    low = lax.broadcasted_iota(jnp.int32, (16, 128), 1) < 64
    for term in range(2):
        for t in range(4):
            now = times[t]
            for pair in range(2):
                v = []
                for k in range(2):
                    tb = 2 * pair + k
                    value = raw[term, t, tb].astype(jnp.float32)
                    v.append(jnp.where(hist * 4 + tb <= now, value, jnp.zeros_like(value)))
                depth = slice(128 * pair, 128 * pair + 128)
                re = jnp.where(low, v[0], pltpu.roll(v[1], 64, 1))
                im = jnp.where(low, pltpu.roll(v[0], 64, 1), v[1])
                left[term, 0, 16 * t : 16 * t + 16, depth] = re.astype(jnp.bfloat16)
                left[term, 0, 64 + 16 * t : 80 + 16 * t, depth] = im.astype(jnp.bfloat16)

    sign = jnp.where(lax.broadcasted_iota(jnp.int32, (64, 128), 1) < 64, -1.0, 1.0).astype(jnp.float32)

    def products(first_stage, n, first_col, target, masked):
        def two(j, carry):
            rights = []
            for term in range(2):
                columns = []
                for k in range(2):
                    c = first_col + 2 * j + k
                    rows = []
                    for tb in range(4):
                        g = green[term, tb, c]
                        if not masked:
                            g = jnp.where(hist * 4 + tb >= starts[c], g, jnp.zeros_like(g))
                            green[term, tb, c] = g
                        rows.append(g)
                    columns.append(jnp.concatenate(rows, axis=0))
                rights.append(jnp.concatenate(columns, axis=1))
            acc = None
            for term in range(2):
                lhs = left[term, first_stage : first_stage + n].reshape(n * 128, 256)
                d = jnp.dot(lhs, rights[term], preferred_element_type=jnp.float32)
                acc = d if acc is None else acc + d
            for i in range(n):
                for k in range(2):
                    one = acc[128 * i : 128 * i + 64, 128 * k : 128 * k + 128]
                    two_ = acc[128 * i + 64 : 128 * i + 128, 128 * k : 128 * k + 128]
                    value = one + pltpu.roll(two_, 64, 1) * sign
                    target[first_stage + i, 2 * j + k] = value.reshape(4, 16, 128)
            return carry

        lax.fori_loop(0, COLS // 2, two, 0, unroll=COLS // 2)

    def peers(send):
        def one(i, carry):
            send(4 + (i + 1) // 2 * (1 - 2 * (i % 2)))
            return carry

        lax.fori_loop(0, RING - 1, one, 0)

    def pair_copy(s, n):
        at = pl.ds(s, n)
        return remote(c_send.at[at], c_recv.at[at], c_s.at[s], c_r.at[s], sibling)

    def encode(s):
        def add(c, most):
            v = part[s, c] + c_recv[s, c]
            part[s, c] = v
            return jnp.maximum(most, jnp.max(jnp.abs(v).reshape(8, 8, 128), axis=0))

        most = lax.fori_loop(0, COLS, add, jnp.zeros((8, 128), jnp.float32))
        most = jnp.maximum(jnp.max(most, axis=0, keepdims=True), 1e-33)
        scale[s] = most * (1.0 / 32767.0)
        factor = (32767.0 / most).reshape(1, 1, 128)

        def code(c, carry):
            coded[s, c] = jnp.round(part[s, c] * factor).astype(jnp.int32).astype(jnp.int16)
            return carry

        lax.fori_loop(0, COLS, code, 0)

    def ring_one(s):
        def send(d):
            i = (a + d) % RING
            remote(coded.at[s, i], rx_p.at[s, d - 1], r1_s.at[s, 0], r1_r.at[s, 0], at_a(i)).start()
            remote(scale.at[s], sc_p.at[s, d - 1], k_s.at[s, 0], k_r.at[s, 0], at_a(i)).start()
            i = (b + d) % RING
            remote(coded.at[s, 8 + i // 2, pl.ds(2 * (i % 2), 2)], rx_q.at[s, d - 1], r1_s.at[s, 1], r1_r.at[s, 1], at_b(i)).start()
            remote(scale.at[s], sc_q.at[s, d - 1], k_s.at[s, 1], k_r.at[s, 1], at_b(i)).start()

        peers(send)

    def ring_one_all(s):
        return [
            remote(rx_p.at[s], rx_p.at[s], r1_s.at[s, 0], r1_r.at[s, 0], sibling),
            remote(sc_p.at[s], sc_p.at[s], k_s.at[s, 0], k_r.at[s, 0], sibling),
            remote(rx_q.at[s], rx_q.at[s], r1_s.at[s, 1], r1_r.at[s, 1], sibling),
            remote(sc_q.at[s], sc_q.at[s], k_s.at[s, 1], k_r.at[s, 1], sibling),
        ]

    def wide(codes, factor):
        return codes.astype(jnp.int32).astype(jnp.float32) * factor.reshape(1, 1, 128)

    def codes_of(total, codes, factor):
        most = jnp.max(jnp.abs(total).reshape(-1, 128), axis=0, keepdims=True)
        most = jnp.maximum(most, 1e-33)
        factor[...] = most * (1.0 / 32767.0)
        codes[...] = jnp.round(total * (32767.0 / most).reshape(1, 1, 128)).astype(jnp.int32).astype(jnp.int16)

    def ring_two(s):
        take(("one", s))
        total = part[s, a]
        for d in range(RING - 1):
            total = total + wide(rx_p[s, d], sc_p[s, d])
        codes_of(total, xp.at[s, b], kp.at[s, b])
        total = part[s, 8 + b // 2, pl.ds(2 * (b % 2), 2)]
        for d in range(RING - 1):
            total = total + wide(rx_q[s, d], sc_q[s, d])
        codes_of(total, xq.at[s, a], kq.at[s, a])

        def send(d):
            to = at_b((b + d) % RING)
            remote(xp.at[s, b], xp.at[s, b], r2_s.at[s, 0], r2_r.at[s, 0], to).start()
            remote(kp.at[s, b], kp.at[s, b], k2_s.at[s, 0], k2_r.at[s, 0], to).start()
            to = at_a((a + d) % RING)
            remote(xq.at[s, a], xq.at[s, a], r2_s.at[s, 1], r2_r.at[s, 1], to).start()
            remote(kq.at[s, a], kq.at[s, a], k2_s.at[s, 1], k2_r.at[s, 1], to).start()

        peers(send)
        copies = []
        for n, (codes, factors) in enumerate(((xp, kp), (xq, kq))):
            c, f = codes.at[s, pl.ds(0, 7)], factors.at[s, pl.ds(0, 7)]
            copies.append(remote(c, c, r2_s.at[s, n], r2_r.at[s, n], sibling))
            copies.append(remote(f, f, k2_s.at[s, n], k2_r.at[s, n], sibling))
        arrivals["two", s] = lambda: [copy.wait_recv() for copy in copies]
        departures.extend(copy.wait_send for copy in copies)

    def rows_of(s):
        return (x + STEP[s]) % 4

    def spread(s):
        take(("two", s))
        total = wide(xp[s, 0], kp[s, 0])
        for d in range(1, RING):
            total = total + wide(xp[s, d], kp[s, d])
        mine = out.at[:, a, rows_of(s)]
        mine[...] = total.astype(jnp.bfloat16)
        total = wide(xq[s, 0], kq[s, 0])
        for d in range(1, RING):
            total = total + wide(xq[s, d], kq[s, d])
        my_q = out.at[pl.ds(2 * (b % 2), 2), 8 + b // 2, rows_of(s)]
        my_q[...] = total.astype(jnp.bfloat16)

        def send(d):
            remote(mine, mine, a2_s.at[s, 0], a2_r.at[s, 0], at_a((a + d) % RING)).start()
            remote(my_q, my_q, a2_s.at[s, 1], a2_r.at[s, 1], at_b((b + d) % RING)).start()

        peers(send)
        arrivals["all", s] = lambda: [copy.wait_recv() for copy in spread_all(s)]
        departures.extend(copy.wait_send for copy in spread_all(s))

    def spread_all(s):
        p = out.at[:, pl.ds(0, 7), rows_of(s)]
        q = out.at[pl.ds(0, 2), pl.ds(0, 7), rows_of(s)]
        return [remote(p, p, a2_s.at[s, 0], a2_r.at[s, 0], sibling), remote(q, q, a2_s.at[s, 1], a2_r.at[s, 1], sibling)]

    def hand_over(s):
        mine = out.at[:, :, rows_of(s)]
        place = out_ref.at[:, pl.ds(base, COLS), rows_of(s)]
        return remote(mine, place, f_s.at[s], f_r.at[s], sibling), pltpu.make_async_copy(mine, place, l_s.at[s])

    def forward(s):
        take(("all", s))
        there, here = hand_over(s)
        there.start()
        here.start()
        arrivals["out", s] = there.wait_recv
        departures.append(there.wait_send)
        departures.append(here.wait)

    def quarter(stage):
        return remote(left.at[:, 0], left.at[:, stage], x_s.at[stage - 1], x_r.at[stage - 1], at_x((x + 4 - STEP[stage]) % 4))

    arrivals, departures = {}, []

    def take(key):
        arrivals.pop(key)()

    def start_quarter(stage):
        quarter(stage).start()
        arrivals["x", stage] = quarter(stage).wait_recv
        departures.append(quarter(stage).wait_send)

    def start_pair(s, n):
        pair_copy(s, n).start()
        arrivals["pair", s] = pair_copy(s, n).wait_recv
        departures.append(pair_copy(s, n).wait_send)

    def first_half():
        loads[2].wait()
        loads[3].wait()
        products(0, 1, other, c_send, False)

    def second_half():
        loads[4].wait()
        loads[5].wait()
        products(0, 1, base, part, False)

    def sums(s, n):
        take(("pair", s))
        for k in range(s, s + n):
            encode(k)
            ring_one(k)
            arrivals["one", k] = lambda k=k: [copy.wait_recv() for copy in ring_one_all(k)]
            departures.extend(copy.wait_send for copy in ring_one_all(k))

    steps = [
        first_half,
        lambda: pl.semaphore_wait(barrier, 18),
        lambda: (start_quarter(1), start_quarter(2)),
        lambda: start_pair(0, 1),
        second_half,
        lambda: start_quarter(3),
        lambda: sums(0, 1),
        lambda: (take(("x", 1)), take(("x", 2))),
        lambda: products(1, 2, other, c_send, True),
        lambda: start_pair(1, 2),
        lambda: products(1, 2, base, part, True),
        lambda: sums(1, 2),
        lambda: ring_two(0),
        lambda: take(("x", 3)),
        lambda: products(3, 1, other, c_send, True),
        lambda: start_pair(3, 1),
        lambda: products(3, 1, base, part, True),
        lambda: sums(3, 1),
        lambda: ring_two(1),
        lambda: spread(0),
        lambda: ring_two(2),
        lambda: ring_two(3),
        lambda: spread(1),
        lambda: forward(0),
        lambda: spread(2),
        lambda: spread(3),
        lambda: forward(1),
        lambda: forward(2),
        lambda: forward(3),
    ]
    for step in steps:
        step()
    for wait in list(arrivals.values()) + departures:
        wait()


def on_device(sigma_ret, sigma_less, green_less, green_adv, time_now, col_start):
    dma = pltpu.SemaphoreType.DMA
    f32, bf16, i16 = jnp.float32, jnp.bfloat16, jnp.int16
    out = pl.pallas_call(
        kernel,
        out_shape=jax.ShapeDtypeStruct((4, 24, 4, 16, 128), bf16),
        in_specs=[pl.BlockSpec(memory_space=pl.ANY)] * 6,
        out_specs=pl.BlockSpec(memory_space=pl.ANY),
        scratch_shapes=[
            pltpu.SMEM((4,), jnp.int32),
            pltpu.SMEM((24,), jnp.int32),
            pltpu.VMEM((2, 4, 4, 16, 128), bf16),
            pltpu.VMEM((2, 4, 128, 256), bf16),
            pltpu.VMEM((2, 4, 24, 64, 128), bf16),
            pltpu.VMEM((4, COLS, 4, 16, 128), bf16),
            pltpu.VMEM((4, COLS, 4, 16, 128), f32),
            pltpu.VMEM((4, COLS, 4, 16, 128), f32),
            pltpu.VMEM((4, COLS, 4, 16, 128), f32),
            pltpu.VMEM((4, COLS, 4, 16, 128), i16),
            pltpu.VMEM((4, 1, 128), f32),
            pltpu.VMEM((4, 7, 4, 16, 128), i16),
            pltpu.VMEM((4, 7, 2, 16, 128), i16),
            pltpu.VMEM((4, 7, 1, 128), f32),
            pltpu.VMEM((4, 7, 1, 128), f32),
            pltpu.VMEM((4, 8, 4, 16, 128), i16),
            pltpu.VMEM((4, 8, 2, 16, 128), i16),
            pltpu.VMEM((4, 8, 1, 128), f32),
            pltpu.VMEM((4, 8, 1, 128), f32),
            dma((8,)),
            dma((3,)), dma((3,)),
            dma((4,)), dma((4,)),
            dma((4, 2)), dma((4, 2)),
            dma((4, 2)), dma((4, 2)),
            dma((4, 2)), dma((4, 2)), dma((4, 2)), dma((4, 2)),
            dma((4, 2)), dma((4, 2)),
            dma((4,)), dma((4,)), dma((4,)),
        ],
        compiler_params=pltpu.CompilerParams(collective_id=0, has_side_effects=True, vmem_limit_bytes=61000 * 1024),
        cost_estimate=pl.CostEstimate(flops=1_610_612_736, bytes_accessed=5_000_000, transcendentals=0),
    )(time_now, col_start, sigma_ret, sigma_less, green_less, green_adv)
    return out.reshape(4, 24, 64, 128)


def solution(mesh):
    return jax.shard_map(
        on_device,
        mesh=mesh,
        in_specs=(
            P(None, "hist", "col", None),
            P(None, "hist", "col", None),
            P("hist", "col", None, None),
            P("hist", "col", None, None),
            P(),
            P("col"),
        ),
        out_specs=P(None, "col", None, None),
        check_vma=False,
    )
```

```python
import functools

import jax
import jax.numpy as jnp
from jax import lax
from jax.experimental import pallas as pl
from jax.experimental.pallas import tpu as pltpu
from jax.sharding import PartitionSpec as P

MESH = pl.DeviceIdType.MESH
RING = 8
PIECES = 4
COLS = 12
OWNED = (0, 1)


def kernel(time_ref, start_ref, sr_ref, sl_ref, gl_ref, ga_ref, out_ref,
           times, starts, raw, left, green, out, c_send, c_recv, part, coded, scale, rx_p, rx_q, sc_p, sc_q, sum_p, sum_q, own_p, own_q, xp, xq, kp, kq,
           in_sem, x_s, x_r, c_s, c_r, r1_s, r1_r, k_s, k_r, r2p_s, r2q_s, r2p_r, r2q_r, r2_s, r2_r, k2_s, k2_r,
           a1p_s, a1q_s, a1p_r, a1q_r, a2_s, a2_r, f_s, f_r, l_s):
    hist, x = lax.axis_index("hist"), lax.axis_index("col")
    core = hist % 2
    z, y = hist // 16, (hist // 2) % 8
    a = y * (1 - core) + z * core
    b = z * (1 - core) + y * core
    step_a, step_b = 2 + 14 * core, 16 - 14 * core
    base = COLS * core
    other = COLS * (1 - core)

    peers_a, peers_b = [], []
    for d in (4, 3, 5, 2, 6, 1, 7):
        pos = lax.rem(a + d, RING)
        peers_a.append((d, pos, (pos * step_a + b * step_b + core, x)))
        pos = lax.rem(b + d, RING)
        peers_b.append((d, pos, (a * step_a + pos * step_b + core, x)))

    def at_x(pos):
        return (hist, pos)

    sibling = (hist + 1 - 2 * core, x)

    def remote(src, dst, send, recv, device):
        return pltpu.make_async_remote_copy(
            src_ref=src, dst_ref=dst, send_sem=send, recv_sem=recv, device_id=device, device_id_type=MESH
        )

    barrier = pltpu.get_barrier_semaphore()
    for device in [d[2] for pair in zip(peers_a, peers_b) for d in pair] + [at_x(lax.rem(x + j, 4)) for j in (2, 1, 3)] + [sibling]:
        pl.semaphore_signal(barrier, inc=1, device_id=device, device_id_type=MESH)

    small = [
        pltpu.make_async_copy(time_ref, times, in_sem.at[6]),
        pltpu.make_async_copy(start_ref, starts, in_sem.at[7]),
    ]
    loads = [pltpu.make_async_copy(sr_ref, raw.at[0], in_sem.at[0]), pltpu.make_async_copy(sl_ref, raw.at[1], in_sem.at[1])]
    for half, first in ((0, other), (1, base)):
        for term, ref in ((0, gl_ref), (1, ga_ref)):
            columns = pl.ds(first, COLS)
            loads.append(pltpu.make_async_copy(ref.at[:, columns], green.at[term, :, columns], in_sem.at[2 + 2 * half + term]))
    for load in loads[:2] + small + loads[2:]:
        load.start()

    for load in loads[:2] + small:
        load.wait()
    low = lax.broadcasted_iota(jnp.int32, (16, 128), 1) < 64
    for term in range(2):
        for t in range(4):
            now = times[t]
            for pair in range(2):
                v = []
                for k in range(2):
                    tb = 2 * pair + k
                    value = raw[term, t, tb].astype(jnp.float32)
                    v.append(jnp.where(hist * 4 + tb <= now, value, jnp.zeros_like(value)))
                depth = slice(128 * pair, 128 * pair + 128)
                re = jnp.where(low, v[0], pltpu.roll(v[1], 64, 1))
                im = jnp.where(low, pltpu.roll(v[0], 64, 1), v[1])
                left[0, term, 0, t, :, depth] = re.astype(jnp.bfloat16)
                left[0, term, 1, t, :, depth] = im.astype(jnp.bfloat16)

    sign = jnp.where(lax.broadcasted_iota(jnp.int32, (64, 128), 1) < 64, -1.0, 1.0).astype(jnp.float32)

    def products(stage, first_col, target, masked):
        def two(j, carry):
            rights = []
            for term in range(2):
                columns = []
                for k in range(2):
                    c = first_col + 2 * j + k
                    rows = []
                    for tb in range(4):
                        g = green[term, tb, c]
                        if not masked:
                            g = jnp.where(hist * 4 + tb >= starts[c], g, jnp.zeros_like(g))
                            green[term, tb, c] = g
                        rows.append(g)
                    columns.append(jnp.concatenate(rows, axis=0))
                rights.append(jnp.concatenate(columns, axis=1))
            acc = None
            for term in range(2):
                lhs = left[stage, term].reshape(128, 256)
                d = jnp.dot(lhs, rights[term], preferred_element_type=jnp.float32)
                acc = d if acc is None else acc + d
            for k in range(2):
                lanes = slice(128 * k, 128 * k + 128)
                value = acc[:64, lanes] + pltpu.roll(acc[64:, lanes], 64, 1) * sign
                target[2 * j + k, stage] = value.reshape(4, 16, 128)
            return carry

        lax.fori_loop(0, COLS // 2, two, 0, unroll=COLS // 2)

    def pair_copy(s):
        return remote(c_send.at[:, s], c_recv.at[:, s], c_s.at[s], c_r.at[s], sibling)

    def encode(s):
        def add(c, most):
            v = part[c, s] + c_recv[c, s]
            part[c, s] = v
            return jnp.maximum(most, jnp.max(jnp.abs(v).reshape(8, 8, 128), axis=0))

        most = lax.fori_loop(0, COLS, add, jnp.zeros((8, 128), jnp.float32), unroll=2)
        most = jnp.maximum(jnp.max(most, axis=0, keepdims=True), 1e-33)
        scale[s] = most * (1.0 / 32767.0)
        factor = (32767.0 / most).reshape(1, 1, 128)

        def code(c, carry):
            coded[c, s] = jnp.round(part[c, s] * factor).astype(jnp.int32).astype(jnp.int16)
            return carry

        lax.fori_loop(0, COLS, code, 0, unroll=2)

    def ring_one(s):
        for (d, i, to_a), (_, k, to_b) in zip(peers_a, peers_b):
            remote(coded.at[i, s], rx_p.at[s, d - 1], r1_s.at[s, 0], r1_r.at[s, 0], to_a).start()
            mine = coded.at[8 + k // 2, s, pl.ds(2 * (k % 2), 2)]
            remote(mine, rx_q.at[s, d - 1], r1_s.at[s, 1], r1_r.at[s, 1], to_b).start()
            remote(scale.at[s], sc_p.at[s, d - 1], k_s.at[s, 0], k_r.at[s, 0], to_a).start()
            remote(scale.at[s], sc_q.at[s, d - 1], k_s.at[s, 1], k_r.at[s, 1], to_b).start()
        copies = [
            remote(rx_p.at[s], rx_p.at[s], r1_s.at[s, 0], r1_r.at[s, 0], sibling),
            remote(sc_p.at[s], sc_p.at[s], k_s.at[s, 0], k_r.at[s, 0], sibling),
            remote(rx_q.at[s], rx_q.at[s], r1_s.at[s, 1], r1_r.at[s, 1], sibling),
            remote(sc_q.at[s], sc_q.at[s], k_s.at[s, 1], k_r.at[s, 1], sibling),
        ]
        arrivals["one", s] = lambda: [copy.wait_recv() for copy in copies]
        departures.extend(copy.wait_send for copy in copies)

    def wide(codes, factor):
        return codes.astype(jnp.int32).astype(jnp.float32) * factor.reshape(1, 1, 128)

    def codes_of(total, codes, factor):
        most = jnp.max(jnp.abs(total).reshape(-1, 128), axis=0, keepdims=True)
        most = jnp.maximum(most, 1e-33)
        factor[...] = most * (1.0 / 32767.0)
        codes[...] = jnp.round(total * (32767.0 / most).reshape(1, 1, 128)).astype(jnp.int32).astype(jnp.int16)

    def ring_one_sums(s):
        take(("one", s))
        total_p = part[a, s]
        for d in range(RING - 1):
            total_p = total_p + wide(rx_p[s, d], sc_p[s, d])
        total_q = part[8 + b // 2, s, pl.ds(2 * (b % 2), 2)]
        for d in range(RING - 1):
            total_q = total_q + wide(rx_q[s, d], sc_q[s, d])
        return total_p, total_q

    def tile_p(s, k):
        return out.at[a, s, k]

    def tile_q(s, k):
        return out.at[8 + b // 2, s, 2 * (b % 2) + k]

    def to_owners(s):
        sum_p[s], sum_q[s] = ring_one_sums(s)
        u = s // 2
        for k in range(4):
            o = 4 * (s % 2) + k
            to = (a * step_a + o * step_b + core, x)
            copy = remote(sum_p.at[s, k], own_p.at[u, lax.rem(b - o + 15, RING)], r2p_s.at[s, k], r2p_r.at[u], to)
            pl.when(o != b)(copy.start)
            departures.append(functools.partial(pl.when(o != b), copy.wait_send))
        for k in range(2):
            o = 2 * s + k
            to = (o * step_a + b * step_b + core, x)
            copy = remote(sum_q.at[s, k], own_q.at[lax.rem(a - o + 15, RING)], r2q_s.at[s, k], r2q_r.at[0], to)
            pl.when(o != a)(copy.start)
            departures.append(functools.partial(pl.when(o != a), copy.wait_send))
        all_p = remote(own_p.at[u, pl.ds(0, 7)], own_p.at[u, pl.ds(0, 7)], r2p_s.at[s, 0], r2p_r.at[u], sibling)
        all_q = remote(own_q.at[pl.ds(0, 7)], own_q.at[pl.ds(0, 7)], r2q_s.at[s, 0], r2q_r.at[0], sibling)
        arrivals["p", s] = lambda: pl.when(b // 4 == s % 2)(all_p.wait_recv)
        arrivals["q", s] = lambda: pl.when(a // 2 == s)(all_q.wait_recv)

    def own(s):
        u = s // 2
        take(("p", s))

        @pl.when(b // 4 == s % 2)
        def _():
            total = sum_p[s, b % 4]
            for d in range(RING - 1):
                total = total + own_p[u, d]
            tile = tile_p(s, b % 4)
            tile[...] = total.astype(jnp.bfloat16)
            for _, _, to_b in peers_b:
                remote(tile, tile, a1p_s.at[u], a1p_r.at[s, b % 4], to_b).start()

        take(("q", s))

        @pl.when(a // 2 == s)
        def _():
            total = sum_q[s, a % 2]
            for d in range(RING - 1):
                total = total + own_q[d]
            tile = tile_q(s, a % 2)
            tile[...] = total.astype(jnp.bfloat16)
            for _, _, to_a in peers_a:
                remote(tile, tile, a1q_s.at[0], a1q_r.at[s, a % 2], to_a).start()

        seven = out.at[pl.ds(0, 7), 0, 0]
        sent_p = remote(seven, seven, a1p_s.at[u], a1p_r.at[s, 0], sibling)
        sent_q = remote(seven, seven, a1q_s.at[0], a1q_r.at[s, 0], sibling)
        departures.append(functools.partial(pl.when(b // 4 == s % 2), sent_p.wait_send))
        departures.append(functools.partial(pl.when(a // 2 == s), sent_q.wait_send))
        for k in range(4):
            copy = remote(tile_p(s, k), tile_p(s, k), a1p_s.at[0], a1p_r.at[s, k], sibling)
            arrivals["tp", s, k] = functools.partial(pl.when(4 * (s % 2) + k != b), copy.wait_recv)
        for k in range(2):
            copy = remote(tile_q(s, k), tile_q(s, k), a1q_s.at[0], a1q_r.at[s, k], sibling)
            arrivals["tq", s, k] = functools.partial(pl.when(2 * s + k != a), copy.wait_recv)

    def to_all(s):
        total_p, total_q = ring_one_sums(s)
        my_p, my_kp = xp.at[s, b], kp.at[s, b]
        codes_of(total_p, my_p, my_kp)
        my_q, my_kq = xq.at[s, a], kq.at[s, a]
        codes_of(total_q, my_q, my_kq)
        for (_, _, to_a), (_, _, to_b) in zip(peers_a, peers_b):
            remote(my_p, my_p, r2_s.at[s, 0], r2_r.at[s, 0], to_b).start()
            remote(my_q, my_q, r2_s.at[s, 1], r2_r.at[s, 1], to_a).start()
            remote(my_kp, my_kp, k2_s.at[s, 0], k2_r.at[s, 0], to_b).start()
            remote(my_kq, my_kq, k2_s.at[s, 1], k2_r.at[s, 1], to_a).start()
        copies = []
        for m, (codes, factors) in enumerate(((xp, kp), (xq, kq))):
            c, f = codes.at[s, pl.ds(0, 7)], factors.at[s, pl.ds(0, 7)]
            copies.append(remote(c, c, r2_s.at[s, m], r2_r.at[s, m], sibling))
            copies.append(remote(f, f, k2_s.at[s, m], k2_r.at[s, m], sibling))
        arrivals["two", s] = lambda: [copy.wait_recv() for copy in copies]
        departures.extend(copy.wait_send for copy in copies)

    def add_all(s):
        take(("two", s))
        total = wide(xp[s, 0], kp[s, 0])
        for d in range(1, RING):
            total = total + wide(xp[s, d], kp[s, d])
        out[a, s] = total.astype(jnp.bfloat16)
        total = wide(xq[s, 0], kq[s, 0])
        for d in range(1, RING):
            total = total + wide(xq[s, d], kq[s, d])
        out[8 + b // 2, s, pl.ds(2 * (b % 2), 2)] = total.astype(jnp.bfloat16)

    def ring_two(s):
        (to_owners if s in OWNED else to_all)(s)

    def spread(s):
        if s in OWNED:
            for k in range(4):
                take(("tp", s, k))
            for k in range(2):
                take(("tq", s, k))
        else:
            add_all(s)
        mine, my_q = out.at[a, s], out.at[8 + b // 2, s, pl.ds(2 * (b % 2), 2)]
        for (_, _, to_a), (_, _, to_b) in zip(peers_a, peers_b):
            remote(mine, mine, a2_s.at[s, 0], a2_r.at[s, 0], to_a).start()
            remote(my_q, my_q, a2_s.at[s, 1], a2_r.at[s, 1], to_b).start()
        seven_p, seven_q = out.at[pl.ds(0, 7), s], out.at[pl.ds(0, 7), s, pl.ds(0, 2)]
        copies = [
            remote(seven_p, seven_p, a2_s.at[s, 0], a2_r.at[s, 0], sibling),
            remote(seven_q, seven_q, a2_s.at[s, 1], a2_r.at[s, 1], sibling),
        ]
        arrivals["all", s] = lambda: [copy.wait_recv() for copy in copies]
        departures.extend(copy.wait_send for copy in copies)

    def forward(s):
        take(("all", s))
        for k in range(4):
            if s in (0, 3):
                t, quarter = k, x + 2 * (s // 3)
            else:
                t, quarter = 2 * (s - 1) + k % 2, x + 1 + 2 * (k // 2)
            mine = out.at[:, s, k]
            place = out_ref.at[t, pl.ds(base, COLS), lax.rem(quarter, 4)]
            there = remote(mine, place, f_s.at[s, k], f_r.at[s, k], sibling)
            here = pltpu.make_async_copy(mine, place, l_s.at[s, k])
            there.start()
            here.start()
            arrivals["out", s, k] = there.wait_recv
            departures.append(there.wait_send)
            departures.append(here.wait)

    def gather(s):
        if s == 3:
            copies = [remote(left.at[0], left.at[3], x_s.at[4], x_r.at[4], at_x(lax.rem(x + 2, 4)))]
        else:
            copies = []
            for m, ahead in enumerate((3, 1)):
                src = left.at[0, :, :, pl.ds(2 * (s - 1), 2)]
                dst = left.at[s, :, :, pl.ds(2 * m, 2)]
                n = 2 * (s - 1) + m
                copies.append(remote(src, dst, x_s.at[n], x_r.at[n], at_x(lax.rem(x + ahead, 4))))
        for copy in copies:
            copy.start()
        arrivals["x", s] = lambda: [copy.wait_recv() for copy in copies]
        departures.extend(copy.wait_send for copy in copies)

    arrivals, departures = {}, []

    def take(key):
        arrivals.pop(key)()

    def half_one(s):
        if s == 0:
            pl.semaphore_wait(barrier, 18)
            gather(1)
            loads[2].wait()
            loads[3].wait()
        else:
            take(("x", s))
        products(s, other, c_send, s > 0)
        copy = pair_copy(s)
        copy.start()
        arrivals["pair", s] = copy.wait_recv
        departures.append(copy.wait_send)

    def half_two(s):
        if s == 0:
            loads[4].wait()
            loads[5].wait()
        products(s, base, part, s > 0)

    def sums(s):
        take(("pair", s))
        encode(s)
        ring_one(s)

    steps = [
        (half_one, 0), (gather, 2), (half_two, 0), (sums, 0), (gather, 3),
        (half_one, 1), (half_two, 1), (half_one, 2), (sums, 1), (half_two, 2), (sums, 2),
        (ring_two, 0),
        (half_one, 3), (half_two, 3), (sums, 3),
        (ring_two, 1), (own, 0), (ring_two, 2), (ring_two, 3), (own, 1), (spread, 2), (spread, 0), (spread, 3), (spread, 1), (forward, 0), (forward, 2), (forward, 3), (forward, 1),
    ]
    steps = [(step, s) for step, s in steps if step is not own or s in OWNED]
    for step, s in steps:
        step(s)
    for wait in list(arrivals.values()) + departures:
        wait()


def deliver(src, dst, held, arrive, leave):
    each = 4 * 24 // PIECES
    inward, outward = [], []
    for k in range(PIECES):
        at = (k * each // 24, pl.ds(k * each % 24, each))
        inward.append(pltpu.make_async_copy(src.at[at], held.at[at], arrive.at[k]))
        outward.append(pltpu.make_async_copy(held.at[at], dst.at[at], leave.at[k]))
    for copy in inward:
        copy.start()
    for a, b in zip(inward, outward):
        a.wait()
        b.start()
    for copy in outward:
        copy.wait()


def on_device(sigma_ret, sigma_less, green_less, green_adv, time_now, col_start):
    dma = pltpu.SemaphoreType.DMA
    f32, bf16, i16 = jnp.float32, jnp.bfloat16, jnp.int16
    out = pl.pallas_call(
        kernel,
        out_shape=jax.ShapeDtypeStruct((4, 24, 4, 16, 128), bf16),
        in_specs=[pl.BlockSpec(memory_space=pl.ANY)] * 6,
        out_specs=pl.BlockSpec(memory_space=pl.ANY),
        scratch_shapes=[
            pltpu.SMEM((4,), jnp.int32),
            pltpu.SMEM((24,), jnp.int32),
            pltpu.VMEM((2, 4, 4, 16, 128), bf16),
            pltpu.VMEM((4, 2, 2, 4, 16, 256), bf16),
            pltpu.VMEM((2, 4, 24, 64, 128), bf16),
            pltpu.VMEM((COLS, 4, 4, 16, 128), bf16),
            pltpu.VMEM((COLS, 4, 4, 16, 128), f32),
            pltpu.VMEM((COLS, 4, 4, 16, 128), f32),
            pltpu.VMEM((COLS, 4, 4, 16, 128), f32),
            pltpu.VMEM((COLS, 4, 4, 16, 128), i16),
            pltpu.VMEM((4, 1, 128), f32),
            pltpu.VMEM((4, 7, 4, 16, 128), i16),
            pltpu.VMEM((4, 7, 2, 16, 128), i16),
            pltpu.VMEM((4, 7, 1, 128), f32),
            pltpu.VMEM((4, 7, 1, 128), f32),
            pltpu.VMEM((4, 4, 16, 128), f32),
            pltpu.VMEM((4, 2, 16, 128), f32),
            pltpu.VMEM((2, 8, 16, 128), f32),
            pltpu.VMEM((8, 16, 128), f32),
            pltpu.VMEM((4, 8, 4, 16, 128), i16),
            pltpu.VMEM((4, 8, 2, 16, 128), i16),
            pltpu.VMEM((4, 8, 1, 128), f32),
            pltpu.VMEM((4, 8, 1, 128), f32),
            dma((8,)),
            dma((5,)), dma((5,)),
            dma((4,)), dma((4,)),
            dma((4, 2)), dma((4, 2)),
            dma((4, 2)), dma((4, 2)),
            dma((4, 4)), dma((4, 2)), dma((2,)), dma((1,)),
            dma((4, 2)), dma((4, 2)), dma((4, 2)), dma((4, 2)),
            dma((2,)), dma((1,)), dma((4, 4)), dma((4, 2)),
            dma((4, 2)), dma((4, 2)),
            dma((4, 4)), dma((4, 4)), dma((4, 4)),
        ],
        compiler_params=pltpu.CompilerParams(collective_id=0, has_side_effects=True, vmem_limit_bytes=61000 * 1024),
        cost_estimate=pl.CostEstimate(flops=1_610_612_736, bytes_accessed=5_000_000, transcendentals=0),
    )(time_now, col_start, sigma_ret, sigma_less, green_less, green_adv)
    out = out.reshape(4, 24, 64, 128)
    return pl.pallas_call(
        deliver,
        out_shape=jax.ShapeDtypeStruct(out.shape, out.dtype),
        in_specs=[pl.BlockSpec(memory_space=pl.ANY)],
        out_specs=pl.BlockSpec(memory_space=pl.ANY),
        scratch_shapes=[pltpu.VMEM(out.shape, out.dtype), dma((PIECES,)), dma((PIECES,))],
        compiler_params=pltpu.CompilerParams(vmem_limit_bytes=61000 * 1024),
        cost_estimate=pl.CostEstimate(flops=0, bytes_accessed=3_145_728, transcendentals=0),
    )(out)


def solution(mesh):
    return jax.shard_map(
        on_device,
        mesh=mesh,
        in_specs=(
            P(None, "hist", "col", None),
            P(None, "hist", "col", None),
            P("hist", "col", None, None),
            P("hist", "col", None, None),
            P(),
            P("col"),
        ),
        out_specs=P(None, "col", None, None),
        check_vma=False,
    )
```

```python
import functools

import jax
import jax.numpy as jnp
from jax import lax
from jax.experimental import pallas as pl
from jax.experimental.pallas import tpu as pltpu
from jax.sharding import PartitionSpec as P

MESH = pl.DeviceIdType.MESH
RING = 8
PIECES = 4
COLS = 12
OWNED = (0,)


def kernel(time_ref, start_ref, sr_ref, sl_ref, gl_ref, ga_ref, out_ref,
           times, starts, raw, left, green, out, c_send, c_recv, part, coded, scale, rx_p, rx_q, sc_p, sc_q, sum_p, sum_q, own_p, own_q, xp, xq, kp, kq,
           in_sem, x_s, x_r, c_s, c_r, r1_s, r1_r, k_s, k_r, r2p_s, r2q_s, r2p_r, r2q_r, r2_s, r2_r, k2_s, k2_r,
           a1p_s, a1q_s, a1p_r, a1q_r, a2_s, a2_r, f_s, f_r, l_s):
    hist, x = lax.axis_index("hist"), lax.axis_index("col")
    core = hist % 2
    z, y = hist // 16, (hist // 2) % 8
    a = y * (1 - core) + z * core
    b = z * (1 - core) + y * core
    step_a, step_b = 2 + 14 * core, 16 - 14 * core
    base = COLS * core
    other = COLS * (1 - core)

    peers_a, peers_b = [], []
    for d in (4, 3, 5, 2, 6, 1, 7):
        pos = lax.rem(a + d, RING)
        peers_a.append((d, pos, (pos * step_a + b * step_b + core, x)))
        pos = lax.rem(b + d, RING)
        peers_b.append((d, pos, (a * step_a + pos * step_b + core, x)))

    def at_x(pos):
        return (hist, pos)

    sibling = (hist + 1 - 2 * core, x)

    def remote(src, dst, send, recv, device):
        return pltpu.make_async_remote_copy(
            src_ref=src, dst_ref=dst, send_sem=send, recv_sem=recv, device_id=device, device_id_type=MESH
        )

    barrier = pltpu.get_barrier_semaphore()
    for device in [d[2] for pair in zip(peers_a, peers_b) for d in pair] + [at_x(lax.rem(x + j, 4)) for j in (2, 1, 3)] + [sibling]:
        pl.semaphore_signal(barrier, inc=1, device_id=device, device_id_type=MESH)

    small = [
        pltpu.make_async_copy(time_ref, times, in_sem.at[6]),
        pltpu.make_async_copy(start_ref, starts, in_sem.at[7]),
    ]
    loads = [pltpu.make_async_copy(sr_ref, raw.at[0], in_sem.at[0]), pltpu.make_async_copy(sl_ref, raw.at[1], in_sem.at[1])]
    for half, first in ((0, other), (1, base)):
        for term, ref in ((0, gl_ref), (1, ga_ref)):
            columns = pl.ds(first, COLS)
            loads.append(pltpu.make_async_copy(ref.at[:, columns], green.at[term, :, columns], in_sem.at[2 + 2 * half + term]))
    for load in loads[:2] + small + loads[2:]:
        load.start()

    for load in loads[:2] + small:
        load.wait()
    low = lax.broadcasted_iota(jnp.int32, (16, 128), 1) < 64
    for term in range(2):
        for t in range(4):
            now = times[t]
            for pair in range(2):
                v = []
                for k in range(2):
                    tb = 2 * pair + k
                    value = raw[term, t, tb].astype(jnp.float32)
                    v.append(jnp.where(hist * 4 + tb <= now, value, jnp.zeros_like(value)))
                depth = slice(128 * pair, 128 * pair + 128)
                re = jnp.where(low, v[0], pltpu.roll(v[1], 64, 1))
                im = jnp.where(low, pltpu.roll(v[0], 64, 1), v[1])
                left[0, term, 0, t, :, depth] = re.astype(jnp.bfloat16)
                left[0, term, 1, t, :, depth] = im.astype(jnp.bfloat16)

    sign = jnp.where(lax.broadcasted_iota(jnp.int32, (64, 128), 1) < 64, -1.0, 1.0).astype(jnp.float32)

    def products(stage, first_col, target, masked):
        def two(j, carry):
            rights = []
            for term in range(2):
                columns = []
                for k in range(2):
                    c = first_col + 2 * j + k
                    rows = []
                    for tb in range(4):
                        g = green[term, tb, c]
                        if not masked:
                            g = jnp.where(hist * 4 + tb >= starts[c], g, jnp.zeros_like(g))
                            green[term, tb, c] = g
                        rows.append(g)
                    columns.append(jnp.concatenate(rows, axis=0))
                rights.append(jnp.concatenate(columns, axis=1))
            acc = None
            for term in range(2):
                lhs = left[stage, term].reshape(128, 256)
                d = jnp.dot(lhs, rights[term], preferred_element_type=jnp.float32)
                acc = d if acc is None else acc + d
            for k in range(2):
                lanes = slice(128 * k, 128 * k + 128)
                value = acc[:64, lanes] + pltpu.roll(acc[64:, lanes], 64, 1) * sign
                target[2 * j + k, stage] = value.reshape(4, 16, 128)
            return carry

        lax.fori_loop(0, COLS // 2, two, 0, unroll=COLS // 2)

    def pair_copy(s):
        return remote(c_send.at[:, s], c_recv.at[:, s], c_s.at[s], c_r.at[s], sibling)

    def encode(s):
        def add(c, most):
            v = part[c, s] + c_recv[c, s]
            part[c, s] = v
            return jnp.maximum(most, jnp.max(jnp.abs(v).reshape(8, 8, 128), axis=0))

        most = lax.fori_loop(0, COLS, add, jnp.zeros((8, 128), jnp.float32), unroll=2)
        most = jnp.maximum(jnp.max(most, axis=0, keepdims=True), 1e-33)
        scale[s] = most * (1.0 / 32767.0)
        factor = (32767.0 / most).reshape(1, 1, 128)

        def code(c, carry):
            coded[c, s] = jnp.round(part[c, s] * factor).astype(jnp.int32).astype(jnp.int16)
            return carry

        lax.fori_loop(0, COLS, code, 0, unroll=2)

    def ring_one(s):
        for (d, i, to_a), (_, k, to_b) in zip(peers_a, peers_b):
            remote(coded.at[i, s], rx_p.at[s, d - 1], r1_s.at[s, 0], r1_r.at[s, 0], to_a).start()
            mine = coded.at[8 + k // 2, s, pl.ds(2 * (k % 2), 2)]
            remote(mine, rx_q.at[s, d - 1], r1_s.at[s, 1], r1_r.at[s, 1], to_b).start()
            remote(scale.at[s], sc_p.at[s, d - 1], k_s.at[s, 0], k_r.at[s, 0], to_a).start()
            remote(scale.at[s], sc_q.at[s, d - 1], k_s.at[s, 1], k_r.at[s, 1], to_b).start()
        copies = [
            remote(rx_p.at[s], rx_p.at[s], r1_s.at[s, 0], r1_r.at[s, 0], sibling),
            remote(sc_p.at[s], sc_p.at[s], k_s.at[s, 0], k_r.at[s, 0], sibling),
            remote(rx_q.at[s], rx_q.at[s], r1_s.at[s, 1], r1_r.at[s, 1], sibling),
            remote(sc_q.at[s], sc_q.at[s], k_s.at[s, 1], k_r.at[s, 1], sibling),
        ]
        arrivals["one", s] = lambda: [copy.wait_recv() for copy in copies]
        departures.extend(copy.wait_send for copy in copies)

    def wide(codes, factor):
        return codes.astype(jnp.int32).astype(jnp.float32) * factor.reshape(1, 1, 128)

    def codes_of(total, codes, factor):
        most = jnp.max(jnp.abs(total).reshape(-1, 128), axis=0, keepdims=True)
        most = jnp.maximum(most, 1e-33)
        factor[...] = most * (1.0 / 32767.0)
        codes[...] = jnp.round(total * (32767.0 / most).reshape(1, 1, 128)).astype(jnp.int32).astype(jnp.int16)

    def ring_one_sums(s):
        take(("one", s))
        total_p = part[a, s]
        for d in range(RING - 1):
            total_p = total_p + wide(rx_p[s, d], sc_p[s, d])
        total_q = part[8 + b // 2, s, pl.ds(2 * (b % 2), 2)]
        for d in range(RING - 1):
            total_q = total_q + wide(rx_q[s, d], sc_q[s, d])
        return total_p, total_q

    def tile_p(s, k):
        return out.at[a, s, k]

    def tile_q(s, k):
        return out.at[8 + b // 2, s, 2 * (b % 2) + k]

    def to_owners(s):
        sum_p[s], sum_q[s] = ring_one_sums(s)
        u = s // 2
        for k in range(4):
            o = 4 * (s % 2) + k
            to = (a * step_a + o * step_b + core, x)
            copy = remote(sum_p.at[s, k], own_p.at[u, lax.rem(b - o + 15, RING)], r2p_s.at[s, k], r2p_r.at[u], to)
            pl.when(o != b)(copy.start)
            departures.append(functools.partial(pl.when(o != b), copy.wait_send))
        for k in range(2):
            o = 2 * s + k
            to = (o * step_a + b * step_b + core, x)
            copy = remote(sum_q.at[s, k], own_q.at[lax.rem(a - o + 15, RING)], r2q_s.at[s, k], r2q_r.at[0], to)
            pl.when(o != a)(copy.start)
            departures.append(functools.partial(pl.when(o != a), copy.wait_send))
        all_p = remote(own_p.at[u, pl.ds(0, 7)], own_p.at[u, pl.ds(0, 7)], r2p_s.at[s, 0], r2p_r.at[u], sibling)
        all_q = remote(own_q.at[pl.ds(0, 7)], own_q.at[pl.ds(0, 7)], r2q_s.at[s, 0], r2q_r.at[0], sibling)
        arrivals["p", s] = lambda: pl.when(b // 4 == s % 2)(all_p.wait_recv)
        arrivals["q", s] = lambda: pl.when(a // 2 == s)(all_q.wait_recv)

    def own(s):
        u = s // 2
        take(("p", s))

        @pl.when(b // 4 == s % 2)
        def _():
            total = sum_p[s, b % 4]
            for d in range(RING - 1):
                total = total + own_p[u, d]
            tile = tile_p(s, b % 4)
            tile[...] = total.astype(jnp.bfloat16)
            for _, _, to_b in peers_b:
                remote(tile, tile, a1p_s.at[u], a1p_r.at[s, b % 4], to_b).start()

        take(("q", s))

        @pl.when(a // 2 == s)
        def _():
            total = sum_q[s, a % 2]
            for d in range(RING - 1):
                total = total + own_q[d]
            tile = tile_q(s, a % 2)
            tile[...] = total.astype(jnp.bfloat16)
            for _, _, to_a in peers_a:
                remote(tile, tile, a1q_s.at[0], a1q_r.at[s, a % 2], to_a).start()

        seven = out.at[pl.ds(0, 7), 0, 0]
        sent_p = remote(seven, seven, a1p_s.at[u], a1p_r.at[s, 0], sibling)
        sent_q = remote(seven, seven, a1q_s.at[0], a1q_r.at[s, 0], sibling)
        departures.append(functools.partial(pl.when(b // 4 == s % 2), sent_p.wait_send))
        departures.append(functools.partial(pl.when(a // 2 == s), sent_q.wait_send))
        for k in range(4):
            copy = remote(tile_p(s, k), tile_p(s, k), a1p_s.at[0], a1p_r.at[s, k], sibling)
            arrivals["tp", s, k] = functools.partial(pl.when(4 * (s % 2) + k != b), copy.wait_recv)
        for k in range(2):
            copy = remote(tile_q(s, k), tile_q(s, k), a1q_s.at[0], a1q_r.at[s, k], sibling)
            arrivals["tq", s, k] = functools.partial(pl.when(2 * s + k != a), copy.wait_recv)

    def to_all(s):
        total_p, total_q = ring_one_sums(s)
        my_p, my_kp = xp.at[s, b], kp.at[s, b]
        codes_of(total_p, my_p, my_kp)
        my_q, my_kq = xq.at[s, a], kq.at[s, a]
        codes_of(total_q, my_q, my_kq)
        for (_, _, to_a), (_, _, to_b) in zip(peers_a, peers_b):
            remote(my_p, my_p, r2_s.at[s, 0], r2_r.at[s, 0], to_b).start()
            remote(my_q, my_q, r2_s.at[s, 1], r2_r.at[s, 1], to_a).start()
            remote(my_kp, my_kp, k2_s.at[s, 0], k2_r.at[s, 0], to_b).start()
            remote(my_kq, my_kq, k2_s.at[s, 1], k2_r.at[s, 1], to_a).start()
        copies = []
        for m, (codes, factors) in enumerate(((xp, kp), (xq, kq))):
            c, f = codes.at[s, pl.ds(0, 7)], factors.at[s, pl.ds(0, 7)]
            copies.append(remote(c, c, r2_s.at[s, m], r2_r.at[s, m], sibling))
            copies.append(remote(f, f, k2_s.at[s, m], k2_r.at[s, m], sibling))
        arrivals["two", s] = lambda: [copy.wait_recv() for copy in copies]
        departures.extend(copy.wait_send for copy in copies)

    def add_all(s):
        take(("two", s))
        total = wide(xp[s, 0], kp[s, 0])
        for d in range(1, RING):
            total = total + wide(xp[s, d], kp[s, d])
        out[a, s] = total.astype(jnp.bfloat16)
        total = wide(xq[s, 0], kq[s, 0])
        for d in range(1, RING):
            total = total + wide(xq[s, d], kq[s, d])
        out[8 + b // 2, s, pl.ds(2 * (b % 2), 2)] = total.astype(jnp.bfloat16)

    def ring_two(s):
        (to_owners if s in OWNED else to_all)(s)

    def spread(s):
        if s in OWNED:
            for k in range(4):
                take(("tp", s, k))
            for k in range(2):
                take(("tq", s, k))
        else:
            add_all(s)
        mine, my_q = out.at[a, s], out.at[8 + b // 2, s, pl.ds(2 * (b % 2), 2)]
        for (_, _, to_a), (_, _, to_b) in zip(peers_a, peers_b):
            remote(mine, mine, a2_s.at[s, 0], a2_r.at[s, 0], to_a).start()
            remote(my_q, my_q, a2_s.at[s, 1], a2_r.at[s, 1], to_b).start()
        seven_p, seven_q = out.at[pl.ds(0, 7), s], out.at[pl.ds(0, 7), s, pl.ds(0, 2)]
        copies = [
            remote(seven_p, seven_p, a2_s.at[s, 0], a2_r.at[s, 0], sibling),
            remote(seven_q, seven_q, a2_s.at[s, 1], a2_r.at[s, 1], sibling),
        ]
        arrivals["all", s] = lambda: [copy.wait_recv() for copy in copies]
        departures.extend(copy.wait_send for copy in copies)

    def forward(s):
        take(("all", s))
        for k in range(4):
            if s in (0, 3):
                t, quarter = k, x + 2 * (s // 3)
            else:
                t, quarter = 2 * (s - 1) + k % 2, x + 1 + 2 * (k // 2)
            mine = out.at[:, s, k]
            place = out_ref.at[t, pl.ds(base, COLS), lax.rem(quarter, 4)]
            there = remote(mine, place, f_s.at[s, k], f_r.at[s, k], sibling)
            here = pltpu.make_async_copy(mine, place, l_s.at[s, k])
            there.start()
            here.start()
            arrivals["out", s, k] = there.wait_recv
            departures.append(there.wait_send)
            departures.append(here.wait)

    def gather(s):
        if s == 3:
            copies = [remote(left.at[0], left.at[3], x_s.at[4], x_r.at[4], at_x(lax.rem(x + 2, 4)))]
        else:
            copies = []
            for m, ahead in enumerate((3, 1)):
                src = left.at[0, :, :, pl.ds(2 * (s - 1), 2)]
                dst = left.at[s, :, :, pl.ds(2 * m, 2)]
                n = 2 * (s - 1) + m
                copies.append(remote(src, dst, x_s.at[n], x_r.at[n], at_x(lax.rem(x + ahead, 4))))
        for copy in copies:
            copy.start()
        arrivals["x", s] = lambda: [copy.wait_recv() for copy in copies]
        departures.extend(copy.wait_send for copy in copies)

    arrivals, departures = {}, []

    def take(key):
        arrivals.pop(key)()

    def half_one(s):
        if s == 0:
            pl.semaphore_wait(barrier, 18)
            gather(1)
            loads[2].wait()
            loads[3].wait()
        else:
            take(("x", s))
        products(s, other, c_send, s > 0)
        copy = pair_copy(s)
        copy.start()
        arrivals["pair", s] = copy.wait_recv
        departures.append(copy.wait_send)

    def half_two(s):
        if s == 0:
            loads[4].wait()
            loads[5].wait()
        products(s, base, part, s > 0)

    def sums(s):
        take(("pair", s))
        encode(s)
        ring_one(s)

    steps = [
        (half_one, 0), (gather, 2), (half_two, 0), (sums, 0),
        (half_one, 1), (gather, 3), (half_two, 1), (half_one, 2), (sums, 1), (half_two, 2), (sums, 2),
        (ring_two, 0),
        (half_one, 3), (half_two, 3), (sums, 3),
        (ring_two, 1), (own, 0), (ring_two, 2), (ring_two, 3), (spread, 1), (spread, 0), (spread, 2), (spread, 3), (forward, 1), (forward, 0), (forward, 2), (forward, 3),
    ]
    steps = [(step, s) for step, s in steps if step is not own or s in OWNED]
    for step, s in steps:
        step(s)
    for wait in list(arrivals.values()) + departures:
        wait()


def deliver(src, dst, held, arrive, leave):
    each = 4 * 24 // PIECES
    inward, outward = [], []
    for k in range(PIECES):
        at = (k * each // 24, pl.ds(k * each % 24, each))
        inward.append(pltpu.make_async_copy(src.at[at], held.at[at], arrive.at[k]))
        outward.append(pltpu.make_async_copy(held.at[at], dst.at[at], leave.at[k]))
    for copy in inward:
        copy.start()
    for a, b in zip(inward, outward):
        a.wait()
        b.start()
    for copy in outward:
        copy.wait()


def on_device(sigma_ret, sigma_less, green_less, green_adv, time_now, col_start):
    dma = pltpu.SemaphoreType.DMA
    f32, bf16, i16 = jnp.float32, jnp.bfloat16, jnp.int16
    out = pl.pallas_call(
        kernel,
        out_shape=jax.ShapeDtypeStruct((4, 24, 4, 16, 128), bf16),
        in_specs=[pl.BlockSpec(memory_space=pl.ANY)] * 6,
        out_specs=pl.BlockSpec(memory_space=pl.ANY),
        scratch_shapes=[
            pltpu.SMEM((4,), jnp.int32),
            pltpu.SMEM((24,), jnp.int32),
            pltpu.VMEM((2, 4, 4, 16, 128), bf16),
            pltpu.VMEM((4, 2, 2, 4, 16, 256), bf16),
            pltpu.VMEM((2, 4, 24, 64, 128), bf16),
            pltpu.VMEM((COLS, 4, 4, 16, 128), bf16),
            pltpu.VMEM((COLS, 4, 4, 16, 128), f32),
            pltpu.VMEM((COLS, 4, 4, 16, 128), f32),
            pltpu.VMEM((COLS, 4, 4, 16, 128), f32),
            pltpu.VMEM((COLS, 4, 4, 16, 128), i16),
            pltpu.VMEM((4, 1, 128), f32),
            pltpu.VMEM((4, 7, 4, 16, 128), i16),
            pltpu.VMEM((4, 7, 2, 16, 128), i16),
            pltpu.VMEM((4, 7, 1, 128), f32),
            pltpu.VMEM((4, 7, 1, 128), f32),
            pltpu.VMEM((4, 4, 16, 128), f32),
            pltpu.VMEM((4, 2, 16, 128), f32),
            pltpu.VMEM((2, 8, 16, 128), f32),
            pltpu.VMEM((8, 16, 128), f32),
            pltpu.VMEM((4, 8, 4, 16, 128), i16),
            pltpu.VMEM((4, 8, 2, 16, 128), i16),
            pltpu.VMEM((4, 8, 1, 128), f32),
            pltpu.VMEM((4, 8, 1, 128), f32),
            dma((8,)),
            dma((5,)), dma((5,)),
            dma((4,)), dma((4,)),
            dma((4, 2)), dma((4, 2)),
            dma((4, 2)), dma((4, 2)),
            dma((4, 4)), dma((4, 2)), dma((2,)), dma((1,)),
            dma((4, 2)), dma((4, 2)), dma((4, 2)), dma((4, 2)),
            dma((2,)), dma((1,)), dma((4, 4)), dma((4, 2)),
            dma((4, 2)), dma((4, 2)),
            dma((4, 4)), dma((4, 4)), dma((4, 4)),
        ],
        compiler_params=pltpu.CompilerParams(collective_id=0, has_side_effects=True, vmem_limit_bytes=61000 * 1024),
        cost_estimate=pl.CostEstimate(flops=1_610_612_736, bytes_accessed=5_000_000, transcendentals=0),
    )(time_now, col_start, sigma_ret, sigma_less, green_less, green_adv)
    out = out.reshape(4, 24, 64, 128)
    return pl.pallas_call(
        deliver,
        out_shape=jax.ShapeDtypeStruct(out.shape, out.dtype),
        in_specs=[pl.BlockSpec(memory_space=pl.ANY)],
        out_specs=pl.BlockSpec(memory_space=pl.ANY),
        scratch_shapes=[pltpu.VMEM(out.shape, out.dtype), dma((PIECES,)), dma((PIECES,))],
        compiler_params=pltpu.CompilerParams(vmem_limit_bytes=61000 * 1024),
        cost_estimate=pl.CostEstimate(flops=0, bytes_accessed=3_145_728, transcendentals=0),
    )(out)


def solution(mesh):
    return jax.shard_map(
        on_device,
        mesh=mesh,
        in_specs=(
            P(None, "hist", "col", None),
            P(None, "hist", "col", None),
            P("hist", "col", None, None),
            P("hist", "col", None, None),
            P(),
            P("col"),
        ),
        out_specs=P(None, "col", None, None),
        check_vma=False,
    )
```
